32 devices in a mesh: section: 4 (over x, core), dp: 4 (over z), chan: 2 (over y).
Axes of the slice: x: 2, y: 2, z: 4, core: 2. Of those that a mesh axis runs over, the one named last changes fastest.
Arguments:
- feats: bfloat16 [8, 32, 128, 2048], P('dp', None, None, 'chan'), may hold values from -6 to 6
- offsets: int32 [8], P('dp'), may hold values from 0 to 127
- widths: int32 [8], P('dp'), may hold values from 32 to 64
- labels: int32 [8, 32, 128], P('dp'), may hold values from 0 to 19
- dw_kernel: bfloat16 [4, 9, 2048], P('section', None, 'chan'), may hold values from -2 to 2
- pw_weight: bfloat16 [4, 2048, 256], P('section', 'chan'), may hold values from -0.125 to 0.125
- pw_bias: float32 [4, 256], P('section', 'chan'), may hold values from -3 to 3
- proj: bfloat16 [4, 256, 256], P('section', 'chan'), may hold values from -0.1875 to 0.1875
- proj_bias: float32 [256], P('chan'), may hold values from -3 to 3
- upstream: bfloat16 [256, 8, 32, 128], P('chan', 'dp'), may hold values from -6 to 6
Outputs:
- aspp_out: bfloat16 [256, 8, 32, 128], P('chan', 'dp')
- input_grad: bfloat16 [8, 32, 128, 2048], P('dp', 'section', None, 'chan')
- grad_dw: float32 [4, 9, 2048], P('section', None, 'chan')
- grad_pw: float32 [4, 2048, 256], P('section', 'chan')
- grad_pw_bias: float32 [4, 256], P('section', 'chan')
- grad_proj: float32 [4, 256, 256], P('section', 'chan')
- grad_proj_bias: float32 [256], P('chan')
The draws below stay inside these ranges and needn't reach their ends.
All inputs are finite; a program needn't handle non-finite values.
Results may differ from the reference program's by a relative error of at most 0.008.
Values may be sent and summed in bfloat16 or wider, within the bound.
A program may use at most 192 MiB of HBM per device.

```python
import math
import jax
import jax.numpy as jnp
from jax import lax

C = 2048
BR = 256
FW = 128
FH = 32
RATE = 6
FRAMES = 8
N_SECTION = 4


def with_ends(result, key, least, top_value):
    index_at = [jax.random.randint(jax.random.fold_in(key, axis), (), 0, length) for axis, length in enumerate(result.shape)]
    longest = result.shape.index(max(result.shape))
    neighbour = index_at[:longest] + [(index_at[longest] + 1) % result.shape[longest]] + index_at[longest + 1:]
    return result.at[tuple(index_at)].set(least).at[tuple(neighbour)].set(top_value)


def block_scale(rng, extent, cuts, smallest, high):
    level = 1.0
    for axis_at, parts in cuts:
        draws = jax.random.uniform(jax.random.fold_in(jax.random.fold_in(rng, 6), axis_at), (parts,), jnp.float32, smallest / len(cuts), high / len(cuts))
        level = level * jnp.repeat(jnp.exp(draws), extent[axis_at] // parts).reshape((-1,) + (1,) * (len(extent) - 1 - axis_at))
    return level


def gaussian(key, extent, scale, limit, shards=(), kind=jnp.bfloat16):
    array = jax.random.normal(key, extent, jnp.float32) * scale
    if len(shards) > 0:
        array = block_scale(key, extent, shards, -0.22, 0.18) * array
    return jnp.clip(array, min=-limit, max=limit).astype(kind)


def setup_inputs(seed: int = 0) -> dict:
    key_of = jax.random.split(jax.random.key(seed), 11)
    return {
        "feats": gaussian(key_of[0], (FRAMES, FH, FW, C), 1.0, 6.0, ((0, 4), (3, 2))),
        "offsets": with_ends(jax.random.randint(key_of[1], (FRAMES,), 0, FW), jax.random.fold_in(key_of[1], 1), 0, FW - 1).astype(jnp.int32),
        "widths": with_ends(jax.random.randint(key_of[2], (FRAMES,), FW // 4, FW // 2 + 1), jax.random.fold_in(key_of[2], 1), FW // 4, (FW // 2 + 1) - 1).astype(jnp.int32),
        "labels": with_ends(jax.random.randint(key_of[3], (FRAMES, FH, FW), 0, 20), jax.random.fold_in(key_of[3], 1), 0, 19).astype(jnp.int32),
        "dw_kernel": gaussian(key_of[4], (N_SECTION, 9, C), 9 ** -0.5, 2.0, ((0, 4), (2, 2))),
        "pw_weight": gaussian(key_of[5], (N_SECTION, C, BR), C ** -0.5, 0.125, ((0, 4), (1, 2))),
        "pw_bias": gaussian(key_of[6], (N_SECTION, BR), 0.5, 3.0, ((0, 4), (1, 2)), jnp.float32),
        "proj": gaussian(key_of[7], (N_SECTION, BR, BR), (4 * BR) ** -0.5, 0.1875, ((0, 4), (1, 2))),
        "proj_bias": gaussian(key_of[8], (BR,), 0.5, 3.0, ((0, 2),), jnp.float32),
        "upstream": gaussian(key_of[9], (BR, FRAMES, FH, FW), 1.0, 6.0, ((0, 2), (1, 4))),
    }


void_class = 19

def column_band(offsets, widths, col_count):
    columns = jnp.arange(col_count, dtype=jnp.int32)
    return jnp.mod(columns[None, :] - offsets[:, None], col_count) < widths[:, None]

def swish_slope(value):
    sig = jax.nn.sigmoid(value)
    return sig * (1.0 + value * (1.0 - sig))

def reference(feats, offsets, widths, labels, dw_kernel, pw_weight, pw_bias, proj, proj_bias, upstream):
    frame_count, row_count, col_count, chan_count = feats.shape
    keep = column_band(offsets, widths, col_count).astype(jnp.bfloat16)
    masked = feats * keep[:, None, :, None]
    margin = RATE * (N_SECTION - 1)
    padded = jnp.pad(masked, ((0, 0), (margin, margin), (margin, margin), (0, 0)))
    pixel_count = frame_count * row_count * col_count
    labeled = (labels != void_class).reshape(pixel_count).astype(jnp.float32)
    scaling = 1.0 / math.sqrt(pixel_count)
    saved = []
    zsum = jnp.zeros((BR, pixel_count), jnp.float32)
    for segment_index in range(N_SECTION):
        dilation = RATE * segment_index
        kernel = dw_kernel[segment_index].astype(jnp.float32)
        accum = jnp.zeros((frame_count, row_count, col_count, chan_count), jnp.float32)
        for tap_index in range(9):
            row_step = tap_index // 3 - 1
            col_step = tap_index % 3 - 1
            top = margin + dilation * row_step
            left = margin + dilation * col_step
            accum = accum + padded[:, top:top + row_count, left:left + col_count, :].astype(jnp.float32) * kernel[tap_index]
        depth_out = accum.astype(jnp.bfloat16)
        depth_rows = depth_out.reshape(pixel_count, chan_count)
        preact = jnp.dot(pw_weight[segment_index].T, depth_rows.T, preferred_element_type=jnp.float32) + pw_bias[segment_index][:, None]
        branch_act = jax.nn.silu(preact).astype(jnp.bfloat16)
        zsum = zsum + jnp.dot(proj[segment_index].T, branch_act, preferred_element_type=jnp.float32)
        saved.append((depth_out, preact, branch_act))
    zvalue = zsum + proj_bias[:, None]
    aspp_out = jax.nn.silu(zvalue).astype(jnp.bfloat16).reshape(BR, frame_count, row_count, col_count)
    up_rows = upstream.reshape(BR, pixel_count).astype(jnp.float32)
    out_grad = (up_rows * swish_slope(zvalue) * labeled[None, :]).astype(jnp.bfloat16)
    grad_proj_bias = lax.optimization_barrier(jnp.sum(out_grad.astype(jnp.float32), axis=1)) * scaling
    input_sum = jnp.zeros((frame_count, row_count, col_count, chan_count), jnp.float32)
    grads_dw, grads_pw, grads_pwb, grads_proj = ([], [], [], [])
    for segment_index in range(N_SECTION):
        dilation = RATE * segment_index
        kernel = dw_kernel[segment_index].astype(jnp.float32)
        depth_out, preact, branch_act = saved[segment_index]
        depth_rows = depth_out.reshape(pixel_count, chan_count)
        act_grad = jnp.dot(proj[segment_index], out_grad, preferred_element_type=jnp.float32)
        grads_proj.append(jnp.dot(branch_act, out_grad.T, preferred_element_type=jnp.float32) * scaling)
        pre_grad = (act_grad * swish_slope(preact)).astype(jnp.bfloat16)
        grads_pwb.append(lax.optimization_barrier(jnp.sum(pre_grad.astype(jnp.float32), axis=1)) * scaling)
        grads_pw.append(jnp.dot(depth_rows.T, pre_grad.T, preferred_element_type=jnp.float32) * scaling)
        depth_grad = jnp.dot(pre_grad.T, pw_weight[segment_index].T, preferred_element_type=jnp.float32).astype(jnp.bfloat16)
        depth_grad = depth_grad.reshape(frame_count, row_count, col_count, chan_count)
        padded_grad = jnp.pad(depth_grad, ((0, 0), (margin, margin), (margin, margin), (0, 0)))
        depth_f = depth_grad.astype(jnp.float32)
        tap_grads = []
        for tap_index in range(9):
            row_step = tap_index // 3 - 1
            col_step = tap_index % 3 - 1
            top = margin + dilation * row_step
            left = margin + dilation * col_step
            source = padded[:, top:top + row_count, left:left + col_count, :].astype(jnp.float32)
            tap_grads.append(lax.optimization_barrier(jnp.sum(source * depth_f, axis=(0, 1, 2))) * scaling)
            top_back = margin - dilation * row_step
            left_back = margin - dilation * col_step
            shifted = padded_grad[:, top_back:top_back + row_count, left_back:left_back + col_count, :]
            input_sum = input_sum + shifted.astype(jnp.float32) * kernel[tap_index]
        grads_dw.append(jnp.stack(tap_grads))
    input_grad = (input_sum * keep[:, None, :, None].astype(jnp.float32)).astype(jnp.bfloat16)
    return (aspp_out, input_grad, jnp.stack(grads_dw), jnp.stack(grads_pw), jnp.stack(grads_pwb), jnp.stack(grads_proj), grad_proj_bias)
```

```python
import math

import jax
import jax.numpy as jnp
from jax import lax
from jax.experimental import pallas as pl
from jax.experimental.pallas import tpu as pltpu
from jax.sharding import PartitionSpec as P

RATE = 6
BAND = 64
VOID = 19
LANES = 128
VMEM_LIMIT = 56 * 1024 * 1024


def swish_slope(value):
    sig = jax.nn.sigmoid(value)
    return sig * (1.0 + value * (1.0 - sig))


def column_masks(first, step, count, cols):
    place = lax.broadcasted_iota(jnp.int32, (count, LANES), 0) + first
    place = jnp.where(place >= cols, place - cols, place)
    place = jnp.where(place < 0, place + cols, place)
    lower = (place - step >= 0).astype(jnp.float32)
    upper = (place + step < cols).astype(jnp.float32)
    return lower, upper


def forward_kernel(scal, feats, taps, weight, depth, band, pre, masked, doubled, left, right, *, margin, wing):
    rows, cols, chans = feats.shape[1:]
    ext = depth.shape[1]
    off, width, rate = scal[0], scal[1], scal[2]
    groups = [pl.ds(g * LANES, LANES) for g in range(chans // LANES)]

    @pl.when(pl.program_id(0) == 0)
    def _():
        masked[...] = jnp.zeros_like(masked)
        left[...] = jnp.zeros_like(left)
        right[...] = jnp.zeros_like(right)
        pre[...] = jnp.zeros_like(pre)

    inside = (lax.broadcasted_iota(jnp.int32, (BAND, LANES), 0) < width).astype(jnp.float32)

    def fill(h, carry):
        for g, lanes in enumerate(groups):
            row = feats[0, h, :, lanes].astype(jnp.float32)
            doubled[g, 0:cols] = row
            doubled[g, cols:cols + BAND] = row[0:BAND]
            part = doubled[g, pl.ds(off, BAND)] * inside
            masked[margin + h, :, lanes] = part
            band[h, :, lanes] = part.astype(jnp.bfloat16)
        return carry

    lax.fori_loop(0, rows, fill, 0)

    lower, upper = column_masks(off - wing, rate, ext, cols)
    kernel = taps[...].astype(jnp.float32)
    batch = 4 if rows % 4 == 0 else 1

    def row_group(i, carry):
        for k in range(batch):
            h = i * batch + k
            for g in range(chans // LANES):
                lanes = groups[g]
                sources = [masked[h + margin + (t - 1) * rate, :, lanes] for t in range(3)]
                sums = []
                for j in range(3):
                    total = sources[0] * kernel[j:j + 1, g * LANES:(g + 1) * LANES]
                    for t in (1, 2):
                        total = total + sources[t] * kernel[3 * t + j:3 * t + j + 1, g * LANES:(g + 1) * LANES]
                    sums.append(total)
                left[k, g, 2 * wing:2 * wing + BAND] = sums[0]
                right[k, g, wing:wing + BAND] = sums[2]
                from_left = left[k, g, pl.ds(wing - rate, ext)] * lower
                from_right = right[k, g, pl.ds(rate, ext)] * upper
                wings = jnp.zeros((wing, LANES), jnp.float32)
                middle = jnp.concatenate([wings, sums[1], wings], axis=0)
                depth[h, :, lanes] = (from_left + from_right + middle).astype(jnp.bfloat16)
        some = depth[pl.ds(i * batch, batch)].reshape(batch * ext, chans)
        here = pl.ds(pl.multiple_of(i * batch * ext, 16), batch * ext)
        pre[here, :] += jnp.dot(some, weight[...], preferred_element_type=jnp.float32)
        return carry

    lax.fori_loop(0, rows // batch, row_group, 0)


def forward_call(scal, feats, taps, weight, frame, margin, wing):
    rows, cols, chans = feats.shape[1:]
    ext = BAND + 2 * wing
    block = min(256, chans)
    outs = weight.shape[1]
    buffer = 3 * wing + BAND
    return pl.pallas_call(
        lambda *refs: forward_kernel(*refs, margin=margin, wing=wing),
        grid_spec=pltpu.PrefetchScalarGridSpec(
            num_scalar_prefetch=1,
            grid=(chans // block,),
            in_specs=[
                pl.BlockSpec((1, rows, cols, block), lambda c, s: (frame, 0, 0, c)),
                pl.BlockSpec((9, block), lambda c, s: (0, c)),
                pl.BlockSpec((block, outs), lambda c, s: (c, 0)),
            ],
            out_specs=[
                pl.BlockSpec((rows, ext, block), lambda c, s: (0, 0, c)),
                pl.BlockSpec((rows, BAND, block), lambda c, s: (0, 0, c)),
                pl.BlockSpec((rows * ext, outs), lambda c, s: (0, 0)),
            ],
            scratch_shapes=[
                pltpu.VMEM((rows + 2 * margin, BAND, block), jnp.float32),
                pltpu.VMEM((block // LANES, cols + BAND, LANES), jnp.float32),
                pltpu.VMEM((4, block // LANES, buffer, LANES), jnp.float32),
                pltpu.VMEM((4, block // LANES, buffer, LANES), jnp.float32),
            ],
        ),
        out_shape=[
            jax.ShapeDtypeStruct((rows, ext, chans), jnp.bfloat16),
            jax.ShapeDtypeStruct((rows, BAND, chans), jnp.bfloat16),
            jax.ShapeDtypeStruct((rows * ext, outs), jnp.float32),
        ],
        compiler_params=pltpu.CompilerParams(vmem_limit_bytes=VMEM_LIMIT),
        cost_estimate=pl.CostEstimate(
            flops=2 * rows * ext * chans * outs, bytes_accessed=2 * rows * chans * (cols + ext + BAND), transcendentals=0
        ),
        name="depth_pointwise",
    )(scal, feats, taps, weight)


def backward_kernel(scal, grad, weight, taps, band, term, dw, spread, *, margin, wing):
    rows, ext, outs = grad.shape
    chans = weight.shape[0]
    cols = scal[3]
    off, width, rate = scal[0], scal[1], scal[2]
    batch = 4 if rows % 4 == 0 else 1

    @pl.when(pl.program_id(0) == 0)
    def _():
        spread[...] = jnp.zeros_like(spread)

    def product(i, carry):
        some = grad[pl.ds(i * batch, batch)].reshape(batch * ext, outs)
        out = lax.dot_general(some, weight[...], (((1,), (1,)), ((), ())), preferred_element_type=jnp.float32)
        out = out.astype(jnp.bfloat16).astype(jnp.float32).reshape(batch, ext, chans)
        for g in range(chans // LANES):
            spread[g, pl.ds(margin + i * batch, batch)] = out[:, :, g * LANES:(g + 1) * LANES]
        return carry

    lax.fori_loop(0, rows // batch, product, 0)

    lower, upper = column_masks(off, rate, BAND, cols)
    inside = (lax.broadcasted_iota(jnp.int32, (BAND, LANES), 0) < width).astype(jnp.float32)
    kernel = taps[...].astype(jnp.float32)
    valid = (upper * inside, inside, lower * inside)

    for g in range(chans // LANES):
        lanes = pl.ds(g * LANES, LANES)

        def one_row(h, sums):
            here = band[h, :, lanes].astype(jnp.float32)
            total = None
            new = []
            for j in range(3):
                source = here * valid[j] if j != 1 else here
                part = None
                for t in range(3):
                    value = spread[g, h + margin - (t - 1) * rate, pl.ds(wing - (j - 1) * rate, BAND)]
                    new.append(sums[3 * j + t] + (source * value).reshape(BAND // 8, 8, LANES).sum(axis=0))
                    scaled = value * kernel[3 * t + j:3 * t + j + 1, g * LANES:(g + 1) * LANES]
                    part = scaled if part is None else part + scaled
                part = part * valid[j]
                total = part if total is None else total + part
            term[h, :, lanes] = total.astype(jnp.bfloat16)
            return tuple(new)

        start = tuple(jnp.zeros((8, LANES), jnp.float32) for _ in range(9))
        sums = lax.fori_loop(0, rows, one_row, start)
        for t in range(3):
            for j in range(3):
                dw[3 * t + j:3 * t + j + 1, lanes] = jnp.sum(sums[3 * j + t], axis=0, keepdims=True)


def backward_call(scal, grad, weight, taps, band, margin, wing):
    rows, ext, outs = grad.shape
    chans = weight.shape[0]
    block = min(256, chans)
    return pl.pallas_call(
        lambda *refs: backward_kernel(*refs, margin=margin, wing=wing),
        grid_spec=pltpu.PrefetchScalarGridSpec(
            num_scalar_prefetch=1,
            grid=(chans // block,),
            in_specs=[
                pl.BlockSpec((rows, ext, outs), lambda c, s: (0, 0, 0)),
                pl.BlockSpec((block, outs), lambda c, s: (c, 0)),
                pl.BlockSpec((9, block), lambda c, s: (0, c)),
                pl.BlockSpec((rows, BAND, block), lambda c, s: (0, 0, c)),
            ],
            out_specs=[
                pl.BlockSpec((rows, BAND, block), lambda c, s: (0, 0, c)),
                pl.BlockSpec((9, block), lambda c, s: (0, c)),
            ],
            scratch_shapes=[pltpu.VMEM((block // LANES, rows + 2 * margin, ext, LANES), jnp.float32)],
        ),
        out_shape=[
            jax.ShapeDtypeStruct((rows, BAND, chans), jnp.bfloat16),
            jax.ShapeDtypeStruct((9, chans), jnp.float32),
        ],
        compiler_params=pltpu.CompilerParams(vmem_limit_bytes=VMEM_LIMIT),
        cost_estimate=pl.CostEstimate(
            flops=2 * rows * ext * chans * outs, bytes_accessed=8 * rows * chans * BAND, transcendentals=0
        ),
        name="depth_gradients",
    )(scal, grad, weight, taps, band)


def pick(array, index, axis=0):
    return lax.dynamic_index_in_dim(array, index, axis, keepdims=False)


def owner_sum(blocks, axis):
    size, me = lax.axis_size(axis), lax.axis_index(axis)
    total = pick(blocks, me).astype(jnp.float32)
    for k in range(1, size):
        sent = pick(blocks, lax.rem(me + k, size)).astype(jnp.bfloat16)
        total = total + lax.ppermute(sent, axis, [(i, (i + k) % size) for i in range(size)]).astype(jnp.float32)
    return total


def trade(blocks, axis):
    size, me = lax.axis_size(axis), lax.axis_index(axis)
    result = blocks
    for k in range(1, size):
        sent = pick(blocks, lax.rem(me + k, size))
        got = lax.ppermute(sent, axis, [(i, (i + k) % size) for i in range(size)])
        result = lax.dynamic_update_index_in_dim(result, got, lax.rem(me + size - k, size), 0)
    return result


def gather(block, axis):
    size, me = lax.axis_size(axis), lax.axis_index(axis)
    if size == 2:
        got = lax.ppermute(block, axis, [(0, 1), (1, 0)])
        return jnp.where(me == 0, jnp.stack([block, got]), jnp.stack([got, block]))
    return lax.all_gather(block, axis)


def halving_sum(blocks, axis):
    size, me = lax.axis_size(axis), lax.axis_index(axis)
    shape = blocks.shape[1:]
    bit = 1
    while bit < size:
        blocks = blocks.reshape((blocks.shape[0] // 2, 2) + shape)
        mine = lax.rem(me // bit, 2)
        sent = pick(blocks, 1 - mine, 1).astype(jnp.bfloat16)
        got = lax.ppermute(sent, axis, [(i, i ^ bit) for i in range(size)])
        blocks = pick(blocks, mine, 1).astype(jnp.float32) + got.astype(jnp.float32)
        bit *= 2
    return blocks[0]


def doubling_gather(block, axis):
    size, me = lax.axis_size(axis), lax.axis_index(axis)
    shape = block.shape
    block = block[None]
    bit = size // 2
    while bit:
        got = lax.ppermute(block, axis, [(i, i ^ bit) for i in range(size)])
        mine = lax.rem(me // bit, 2)
        both = jnp.where(mine == 0, jnp.stack([block, got], 1), jnp.stack([got, block], 1))
        block = both.reshape((2 * block.shape[0],) + shape)
        bit //= 2
    return block


def rolled(array, start, axis):
    length = array.shape[axis]
    return lax.dynamic_slice_in_dim(jnp.concatenate([array, array], axis), start, length, axis)


def local(feats, offsets, widths, labels, dw_kernel, pw_weight, pw_bias, proj, proj_bias, upstream):
    frames, rows, cols, chans = feats.shape
    sections, parts = lax.axis_size("section"), lax.axis_size("chan")
    section, part = lax.axis_index("section"), lax.axis_index("chan")
    rate = (RATE * section).astype(jnp.int32)
    margin = RATE * (sections - 1)
    wing = -(-margin // 8) * 8
    ext = BAND + 2 * wing
    share = pw_bias.shape[1]
    branch = share * parts
    scaling = 1.0 / math.sqrt(frames * rows * cols * lax.axis_size("dp"))
    rows_own = rows // parts
    pixels = rows_own * cols
    piece = pixels // sections
    taps, weight = dw_kernel[0], pw_weight[0]

    proj_all = lax.all_gather(proj[0], "chan", axis=0, tiled=True)
    biases = lax.all_gather(jnp.stack([pw_bias[0], proj_bias]), "chan", axis=1, tiled=True)
    pw_bias_all, proj_bias_all = biases[0], biases[1]

    starts = [lax.rem(offsets[f] + (cols - wing), cols) for f in range(frames)]
    scals = [jnp.stack([offsets[f], widths[f], rate, jnp.int32(cols)]) for f in range(frames)]

    ups, labeled = [], []
    for f in range(frames):
        up = rolled(upstream[:, f], starts[f], 2).reshape(share, parts, sections, piece)
        up = pick(up, section, 2).transpose(1, 0, 2)
        ups.append(trade(up, "chan").reshape(branch, piece).T)
        marks = rolled(labels[f], starts[f], 1).reshape(parts, sections, piece)
        labeled.append((pick(pick(marks, part), section) != VOID).astype(jnp.float32))

    firsts = [forward_call(scals[f], feats, taps, weight, f, margin, wing) for f in range(frames)]

    results, terms = [], []
    dw_sum = pw_sum = proj_sum = pw_bias_sum = proj_bias_sum = 0.0
    for f in range(frames):
        depth, band, pre = firsts[f]
        own = owner_sum(pre.reshape(parts, rows_own * ext, branch), "chan") + pw_bias_all
        rest = jnp.broadcast_to(pw_bias_all, (rows_own, cols - ext, branch))
        preact = jnp.concatenate([own.reshape(rows_own, ext, branch), rest], axis=1).reshape(pixels, branch)
        act = jax.nn.silu(preact).astype(jnp.bfloat16)
        zpart = jnp.dot(act, proj_all, preferred_element_type=jnp.float32)
        zvalue = halving_sum(zpart.reshape(sections, piece, branch), "section") + proj_bias_all
        result = jax.nn.silu(zvalue).astype(jnp.bfloat16)
        out_grad = ups[f].astype(jnp.float32) * swish_slope(zvalue) * labeled[f][:, None]
        out_grad = doubling_gather(out_grad.astype(jnp.bfloat16), "section").reshape(pixels, branch)

        act_grad = lax.dot_general(out_grad, proj_all, (((1,), (1,)), ((), ())), preferred_element_type=jnp.float32)
        pre_grad = (act_grad * swish_slope(preact)).astype(jnp.bfloat16)
        sent = pre_grad.reshape(rows_own, cols, branch)[:, :ext]
        grad_rows = gather(sent, "chan").reshape(rows, ext, branch)
        term, dw = backward_call(scals[f], grad_rows, weight, taps, band, margin, wing)
        own_rows = halving_sum(term.reshape(sections, rows // sections, BAND, chans), "section")
        own_rows = jnp.pad(own_rows.astype(jnp.bfloat16), ((0, 0), (0, cols - BAND), (0, 0)))
        terms.append(rolled(own_rows, lax.rem(cols - offsets[f], cols), 1))

        swapped = trade(result.reshape(piece, parts, share).transpose(1, 2, 0), "chan")
        whole = doubling_gather(swapped, "section").transpose(2, 1, 0, 3).reshape(share, rows, cols)
        results.append(rolled(whole, lax.rem(cols - starts[f], cols), 2))

        dw_sum = dw_sum + dw
        pw_sum = pw_sum + lax.dot_general(
            depth.reshape(rows * ext, chans), grad_rows.reshape(rows * ext, branch),
            (((0,), (0,)), ((), ())), preferred_element_type=jnp.float32,
        )
        proj_sum = proj_sum + lax.dot_general(
            act, out_grad, (((0,), (0,)), ((), ())), preferred_element_type=jnp.float32
        )
        pw_bias_sum = pw_bias_sum + jnp.sum(pre_grad.astype(jnp.float32), axis=0)
        proj_bias_sum = proj_bias_sum + jnp.sum(out_grad.astype(jnp.float32), axis=0)

    shared = jnp.concatenate([proj_sum, pw_bias_sum[None], proj_bias_sum[None]], axis=0) * scaling
    shared = lax.psum(shared, ("chan", "dp"))
    kernel_grad, weight_grad = lax.psum((dw_sum * scaling, pw_sum * scaling), "dp")
    mine = part * share
    return (
        jnp.stack(results, 1),
        jnp.stack(terms, 0),
        kernel_grad[None],
        weight_grad[None],
        lax.dynamic_slice_in_dim(shared[branch], mine, share)[None],
        lax.dynamic_slice_in_dim(shared, mine, share, 0)[None],
        lax.dynamic_slice_in_dim(shared[branch + 1], mine, share),
    )


def solution(mesh):
    in_specs = (
        P("dp", None, None, "chan"),
        P("dp"),
        P("dp"),
        P("dp", None, None),
        P("section", None, "chan"),
        P("section", "chan", None),
        P("section", "chan"),
        P("section", "chan", None),
        P("chan"),
        P("chan", "dp", None, None),
    )
    out_specs = (
        P("chan", "dp", None, None),
        P("dp", "section", None, "chan"),
        P("section", None, "chan"),
        P("section", "chan", None),
        P("section", "chan"),
        P("section", "chan", None),
        P("chan"),
    )
    return jax.shard_map(local, mesh=mesh, in_specs=in_specs, out_specs=out_specs, check_vma=False)
```

```python
import math

import jax
import jax.numpy as jnp
from jax import lax
from jax.experimental import pallas as pl
from jax.experimental.pallas import tpu as pltpu
from jax.sharding import PartitionSpec as P

RATE = 6
BAND = 64
VOID = 19
LANES = 128
VMEM_LIMIT = 56 * 1024 * 1024


def swish_slope(value):
    sig = jax.nn.sigmoid(value)
    return sig * (1.0 + value * (1.0 - sig))


def column_masks(first, step, count, cols):
    place = lax.broadcasted_iota(jnp.int32, (count, LANES), 0) + first
    place = jnp.where(place >= cols, place - cols, place)
    place = jnp.where(place < 0, place + cols, place)
    lower = (place - step >= 0).astype(jnp.float32)
    upper = (place + step < cols).astype(jnp.float32)
    return lower, upper


def tap_rows(taps, g):
    kernel = taps[:, g * LANES:(g + 1) * LANES].astype(jnp.float32)
    return [jnp.broadcast_to(kernel[t:t + 1], (8, LANES))[None] for t in range(9)]


def forward_kernel(scal, feats, taps, weight, depth, band, pre, masked, doubled, left, middle, right, edges, *, margin, wing, batch):
    rows, cols, chans = feats.shape[1:]
    ext = depth.shape[1]
    off, width, rate = scal[0], scal[1], scal[2]
    groups = [pl.ds(g * LANES, LANES) for g in range(chans // LANES)]

    @pl.when(pl.program_id(0) == 0)
    def _():
        masked[...] = jnp.zeros_like(masked)
        left[...] = jnp.zeros_like(left)
        middle[...] = jnp.zeros_like(middle)
        right[...] = jnp.zeros_like(right)
        pre[...] = jnp.zeros_like(pre)
        lower, upper = column_masks(off - wing, rate, ext, cols)
        edges[0] = lower
        edges[1] = upper

    def fill(i, carry):
        for k in range(batch):
            for g, lanes in enumerate(groups):
                row = feats[0, i * batch + k, :, lanes].astype(jnp.float32)
                doubled[k, g, 0:cols] = row
                doubled[k, g, cols:cols + BAND] = row[0:BAND]
        inside = (lax.broadcasted_iota(jnp.int32, (BAND, LANES), 0) < width).astype(jnp.float32)
        for k in range(batch):
            h = i * batch + k
            for g, lanes in enumerate(groups):
                part = doubled[k, g, pl.ds(off, BAND)] * inside
                masked[g, margin + h] = part
                band[h, :, lanes] = part.astype(jnp.bfloat16)
        return carry

    lax.fori_loop(0, rows // batch, fill, 0)
    kernels = [tap_rows(taps, g) for g in range(len(groups))]

    def row_group(i, carry):
        for k in range(batch):
            h = i * batch + k
            for g in range(len(groups)):
                for u in range(0, BAND, 16):
                    sources = [
                        masked[g, h + margin + (t - 1) * rate, u:u + 16].reshape(2, 8, LANES) for t in range(3)
                    ]
                    sums = []
                    for j in range(3):
                        total = sources[0] * kernels[g][j]
                        for t in (1, 2):
                            total = total + sources[t] * kernels[g][3 * t + j]
                        sums.append(total.reshape(16, LANES))
                    left[k, g, 2 * wing + u:2 * wing + u + 16] = sums[0]
                    middle[k, g, wing + u:wing + u + 16] = sums[1]
                    right[k, g, wing + u:wing + u + 16] = sums[2]
        for k in range(batch):
            h = i * batch + k
            for g, lanes in enumerate(groups):
                for e in range(0, ext, 16):
                    from_left = left[k, g, pl.ds(wing - rate + e, 16)] * edges[0, e:e + 16]
                    from_right = right[k, g, pl.ds(rate + e, 16)] * edges[1, e:e + 16]
                    out = from_left + from_right + middle[k, g, e:e + 16]
                    depth[h, e:e + 16, lanes] = out.astype(jnp.bfloat16)
        some = depth[pl.ds(i * batch, batch)].reshape(batch * ext, chans)
        here = pl.ds(pl.multiple_of(i * batch * ext, 16), batch * ext)
        pre[here, :] += jnp.dot(some, weight[...], preferred_element_type=jnp.float32)
        return carry

    lax.fori_loop(0, rows // batch, row_group, 0)


def forward_call(scal, feats, taps, weight, frame, margin, wing):
    rows, cols, chans = feats.shape[1:]
    ext = BAND + 2 * wing
    block = min(256, chans)
    outs = weight.shape[1]
    buffer = 3 * wing + BAND
    batch = 4 if rows % 4 == 0 else 1
    lanes = block // LANES
    return pl.pallas_call(
        lambda *refs: forward_kernel(*refs, margin=margin, wing=wing, batch=batch),
        grid_spec=pltpu.PrefetchScalarGridSpec(
            num_scalar_prefetch=1,
            grid=(chans // block,),
            in_specs=[
                pl.BlockSpec((1, rows, cols, block), lambda c, s: (frame, 0, 0, c)),
                pl.BlockSpec((9, block), lambda c, s: (0, c)),
                pl.BlockSpec((block, outs), lambda c, s: (c, 0)),
            ],
            out_specs=[
                pl.BlockSpec((rows, ext, block), lambda c, s: (0, 0, c)),
                pl.BlockSpec((rows, BAND, block), lambda c, s: (0, 0, c)),
                pl.BlockSpec((rows * ext, outs), lambda c, s: (0, 0)),
            ],
            scratch_shapes=[
                pltpu.VMEM((lanes, rows + 2 * margin, BAND, LANES), jnp.float32),
                pltpu.VMEM((batch, lanes, cols + BAND, LANES), jnp.float32),
                pltpu.VMEM((batch, lanes, buffer, LANES), jnp.float32),
                pltpu.VMEM((batch, lanes, ext, LANES), jnp.float32),
                pltpu.VMEM((batch, lanes, buffer, LANES), jnp.float32),
                pltpu.VMEM((2, ext, LANES), jnp.float32),
            ],
        ),
        out_shape=[
            jax.ShapeDtypeStruct((rows, ext, chans), jnp.bfloat16),
            jax.ShapeDtypeStruct((rows, BAND, chans), jnp.bfloat16),
            jax.ShapeDtypeStruct((rows * ext, outs), jnp.float32),
        ],
        compiler_params=pltpu.CompilerParams(vmem_limit_bytes=VMEM_LIMIT),
        cost_estimate=pl.CostEstimate(
            flops=2 * rows * ext * chans * outs, bytes_accessed=2 * rows * chans * (cols + ext + BAND), transcendentals=0
        ),
        name="depth_pointwise",
    )(scal, feats, taps, weight)


def backward_kernel(scal, grad, weight, taps, band, term, dw, spread, valid, *, margin, wing):
    rows, ext, outs = grad.shape
    chans = weight.shape[0]
    cols = scal[3]
    off, width, rate = scal[0], scal[1], scal[2]
    batch = 4 if rows % 4 == 0 else 1

    @pl.when(pl.program_id(0) == 0)
    def _():
        spread[...] = jnp.zeros_like(spread)
        lower, upper = column_masks(off, rate, BAND, cols)
        inside = (lax.broadcasted_iota(jnp.int32, (BAND, LANES), 0) < width).astype(jnp.float32)
        valid[0] = upper * inside
        valid[1] = inside
        valid[2] = lower * inside

    def product(i, carry):
        some = grad[pl.ds(i * batch, batch)].reshape(batch * ext, outs)
        out = lax.dot_general(some, weight[...], (((1,), (1,)), ((), ())), preferred_element_type=jnp.float32)
        out = out.astype(jnp.bfloat16).astype(jnp.float32).reshape(batch, ext, chans)
        for g in range(chans // LANES):
            spread[g, pl.ds(margin + i * batch, batch)] = out[:, :, g * LANES:(g + 1) * LANES]
        return carry

    lax.fori_loop(0, rows // batch, product, 0)

    for g in range(chans // LANES):
        lanes = pl.ds(g * LANES, LANES)
        kernel = tap_rows(taps, g)

        def one_row(h, sums):
            sums = list(sums)
            for u in range(0, BAND, 16):
                here = band[h, u:u + 16, lanes].astype(jnp.float32).reshape(2, 8, LANES)
                total = None
                for j in range(3):
                    mask = valid[j, u:u + 16].reshape(2, 8, LANES)
                    source = here * mask if j != 1 else here
                    part = None
                    for t in range(3):
                        value = spread[g, h + margin - (t - 1) * rate, pl.ds(wing - (j - 1) * rate + u, 16)]
                        value = value.reshape(2, 8, LANES)
                        both = source * value
                        sums[3 * t + j] = sums[3 * t + j] + (both[0] + both[1])
                        scaled = value * kernel[3 * t + j]
                        part = scaled if part is None else part + scaled
                    part = part * mask
                    total = part if total is None else total + part
                term[h, u:u + 16, lanes] = total.reshape(16, LANES).astype(jnp.bfloat16)
            return tuple(sums)

        sums = lax.fori_loop(0, rows, one_row, tuple(jnp.zeros((8, LANES), jnp.float32) for _ in range(9)))
        for t in range(9):
            dw[t:t + 1, lanes] = jnp.sum(sums[t], axis=0, keepdims=True)


def backward_call(scal, grad, weight, taps, band, margin, wing, cut, cuts):
    rows, ext, outs = grad.shape
    chans = weight.shape[0] // cuts
    block = min(256, chans)
    first = cut * (chans // block)
    return pl.pallas_call(
        lambda *refs: backward_kernel(*refs, margin=margin, wing=wing),
        grid_spec=pltpu.PrefetchScalarGridSpec(
            num_scalar_prefetch=1,
            grid=(chans // block,),
            in_specs=[
                pl.BlockSpec((rows, ext, outs), lambda c, s: (0, 0, 0)),
                pl.BlockSpec((block, outs), lambda c, s: (first + c, 0)),
                pl.BlockSpec((9, block), lambda c, s: (0, first + c)),
                pl.BlockSpec((rows, BAND, block), lambda c, s: (0, 0, first + c)),
            ],
            out_specs=[
                pl.BlockSpec((rows, BAND, block), lambda c, s: (0, 0, c)),
                pl.BlockSpec((9, block), lambda c, s: (0, c)),
            ],
            scratch_shapes=[
                pltpu.VMEM((block // LANES, rows + 2 * margin, ext, LANES), jnp.float32),
                pltpu.VMEM((3, BAND, LANES), jnp.float32),
            ],
        ),
        out_shape=[
            jax.ShapeDtypeStruct((rows, BAND, chans), jnp.bfloat16),
            jax.ShapeDtypeStruct((9, chans), jnp.float32),
        ],
        compiler_params=pltpu.CompilerParams(vmem_limit_bytes=VMEM_LIMIT),
        cost_estimate=pl.CostEstimate(
            flops=2 * rows * ext * chans * outs, bytes_accessed=8 * rows * chans * BAND, transcendentals=0
        ),
        name="depth_gradients",
    )(scal, grad, weight, taps, band)


def pick(array, index, axis=0):
    return lax.dynamic_index_in_dim(array, index, axis, keepdims=False)


def owner_sum(blocks, axis):
    size, me = lax.axis_size(axis), lax.axis_index(axis)
    total = pick(blocks, me).astype(jnp.float32)
    for k in range(1, size):
        sent = pick(blocks, lax.rem(me + k, size)).astype(jnp.bfloat16)
        total = total + lax.ppermute(sent, axis, [(i, (i + k) % size) for i in range(size)]).astype(jnp.float32)
    return total


def trade(blocks, axis):
    size, me = lax.axis_size(axis), lax.axis_index(axis)
    result = blocks
    for k in range(1, size):
        sent = pick(blocks, lax.rem(me + k, size))
        got = lax.ppermute(sent, axis, [(i, (i + k) % size) for i in range(size)])
        result = lax.dynamic_update_index_in_dim(result, got, lax.rem(me + size - k, size), 0)
    return result


def gather(block, axis):
    size, me = lax.axis_size(axis), lax.axis_index(axis)
    if size == 2:
        got = lax.ppermute(block, axis, [(0, 1), (1, 0)])
        return jnp.where(me == 0, jnp.stack([block, got]), jnp.stack([got, block]))
    return lax.all_gather(block, axis)


def halving_sum(blocks, axis):
    size, me = lax.axis_size(axis), lax.axis_index(axis)
    shape = blocks.shape[1:]
    bit = 1
    while bit < size:
        blocks = blocks.reshape((blocks.shape[0] // 2, 2) + shape)
        mine = lax.rem(me // bit, 2)
        sent = pick(blocks, 1 - mine, 1).astype(jnp.bfloat16)
        got = lax.ppermute(sent, axis, [(i, i ^ bit) for i in range(size)])
        blocks = pick(blocks, mine, 1).astype(jnp.float32) + got.astype(jnp.float32)
        bit *= 2
    return blocks[0]


def doubling_gather(block, axis):
    size, me = lax.axis_size(axis), lax.axis_index(axis)
    shape = block.shape
    block = block[None]
    bit = size // 2
    while bit:
        got = lax.ppermute(block, axis, [(i, i ^ bit) for i in range(size)])
        mine = lax.rem(me // bit, 2)
        both = jnp.where(mine == 0, jnp.stack([block, got], 1), jnp.stack([got, block], 1))
        block = both.reshape((2 * block.shape[0],) + shape)
        bit //= 2
    return block


def butterfly_sum(value, axis):
    size, bit = lax.axis_size(axis), 1
    while bit < size:
        value = value + lax.ppermute(value, axis, [(i, i ^ bit) for i in range(size)])
        bit *= 2
    return value


def rolled(array, start, axis):
    length = array.shape[axis]
    return lax.dynamic_slice_in_dim(jnp.concatenate([array, array], axis), start, length, axis)


def local(feats, offsets, widths, labels, dw_kernel, pw_weight, pw_bias, proj, proj_bias, upstream):
    frames, rows, cols, chans = feats.shape
    sections, parts = lax.axis_size("section"), lax.axis_size("chan")
    section, part = lax.axis_index("section"), lax.axis_index("chan")
    rate = (RATE * section).astype(jnp.int32)
    margin = RATE * (sections - 1)
    wing = -(-margin // 8) * 8
    ext = BAND + 2 * wing
    share = pw_bias.shape[1]
    branch = share * parts
    scaling = 1.0 / math.sqrt(frames * rows * cols * lax.axis_size("dp"))
    rows_own = rows // parts
    pixels = rows_own * cols
    piece = pixels // sections
    taps, weight = dw_kernel[0], pw_weight[0]

    proj_all = gather(proj[0], "chan").reshape(branch, branch)
    biases = gather(jnp.stack([pw_bias[0], proj_bias]), "chan")
    pw_bias_all, proj_bias_all = biases[:, 0].reshape(branch), biases[:, 1].reshape(branch)

    starts = [lax.rem(offsets[f] + (cols - wing), cols) for f in range(frames)]
    scals = [jnp.stack([offsets[f], widths[f], rate, jnp.int32(cols)]) for f in range(frames)]

    ups, labeled = [], []
    for f in range(frames):
        up = rolled(upstream[:, f], starts[f], 2).reshape(share, parts, sections, piece)
        up = pick(up, section, 2).transpose(1, 0, 2)
        ups.append(trade(up, "chan").reshape(branch, piece).T)
        marks = rolled(labels[f], starts[f], 1).reshape(parts, sections, piece)
        labeled.append((pick(pick(marks, part), section) != VOID).astype(jnp.float32))

    firsts = [forward_call(scals[f], feats, taps, weight, f, margin, wing) for f in range(frames)]

    kept, grads, outs = [], [], []
    proj_sum = pw_bias_sum = proj_bias_sum = 0.0
    for f in range(frames):
        depth, band, pre = firsts[f]
        own = owner_sum(pre.reshape(parts, rows_own * ext, branch), "chan") + pw_bias_all
        rest = jnp.broadcast_to(pw_bias_all, (rows_own, cols - ext, branch))
        preact = jnp.concatenate([own.reshape(rows_own, ext, branch), rest], axis=1).reshape(pixels, branch)
        act = jax.nn.silu(preact).astype(jnp.bfloat16)
        zpart = jnp.dot(act, proj_all, preferred_element_type=jnp.float32)
        zvalue = halving_sum(zpart.reshape(sections, piece, branch), "section") + proj_bias_all
        outs.append(jax.nn.silu(zvalue).astype(jnp.bfloat16))
        out_grad = ups[f].astype(jnp.float32) * swish_slope(zvalue) * labeled[f][:, None]
        out_grad = doubling_gather(out_grad.astype(jnp.bfloat16), "section").reshape(pixels, branch)
        act_grad = lax.dot_general(out_grad, proj_all, (((1,), (1,)), ((), ())), preferred_element_type=jnp.float32)
        pre_grad = (act_grad * swish_slope(preact)).astype(jnp.bfloat16)
        sent = pre_grad.reshape(rows_own, cols, branch)[:, :ext]
        grads.append(gather(sent, "chan").reshape(rows, ext, branch))
        kept.append((act, out_grad, pre_grad))

    outs, kept, _ = lax.optimization_barrier((outs, kept, grads[-1]))
    pw_sum = 0.0
    for f in range(frames):
        act, out_grad, pre_grad = kept[f]
        pw_sum = pw_sum + lax.dot_general(
            firsts[f][0].reshape(rows * ext, chans), grads[f].reshape(rows * ext, branch),
            (((0,), (0,)), ((), ())), preferred_element_type=jnp.float32,
        )
        proj_sum = proj_sum + lax.dot_general(
            act, out_grad, (((0,), (0,)), ((), ())), preferred_element_type=jnp.float32
        )
        pw_bias_sum = pw_bias_sum + jnp.sum(pre_grad.astype(jnp.float32), axis=0)
        proj_bias_sum = proj_bias_sum + jnp.sum(out_grad.astype(jnp.float32), axis=0)
    proj_rows = owner_sum(proj_sum.reshape(parts, share, branch), "chan")
    bias_rows = jnp.stack([pw_bias_sum, proj_bias_sum]).reshape(2, parts, share).transpose(1, 0, 2)
    bias_rows = owner_sum(bias_rows, "chan")
    bias_rows = jnp.pad(bias_rows, ((0, 6), (0, branch - share)))
    shared = jnp.concatenate([pw_sum, proj_rows, bias_rows], axis=0) * scaling
    if frames > 1:
        grads[-1], shared = lax.optimization_barrier((grads[-1], shared))
    shared = lax.psum(shared, "dp")

    cuts = 2 if chans % 512 == 0 else 1
    terms, dw_sums = [], [0.0] * cuts
    for f in range(frames):
        band, halves = firsts[f][1], []
        for cut in range(cuts):
            term, dw = backward_call(scals[f], grads[f], weight, taps, band, margin, wing, cut, cuts)
            own_rows = halving_sum(term.reshape(sections, rows // sections, BAND, chans // cuts), "section")
            halves.append(own_rows.astype(jnp.bfloat16))
            dw_sums[cut] = dw_sums[cut] + dw
        own_rows = jnp.pad(jnp.concatenate(halves, axis=2), ((0, 0), (0, cols - BAND), (0, 0)))
        terms.append(rolled(own_rows, lax.rem(cols - offsets[f], cols), 1))
    kernel_grad = butterfly_sum(jnp.concatenate(dw_sums, axis=1) * scaling, "dp")

    results = []
    for f in range(frames):
        swapped = trade(outs[f].reshape(piece, parts, share).transpose(1, 2, 0), "chan")
        whole = doubling_gather(swapped, "section").transpose(2, 1, 0, 3).reshape(share, rows, cols)
        results.append(rolled(whole, lax.rem(cols - starts[f], cols), 2))

    proj_end = chans + share
    return (
        jnp.stack(results, 1),
        jnp.stack(terms, 0),
        kernel_grad[None],
        shared[None, :chans],
        shared[proj_end:proj_end + 1, :share],
        shared[None, chans:proj_end],
        shared[proj_end + 1, :share],
    )


def solution(mesh):
    in_specs = (
        P("dp", None, None, "chan"),
        P("dp"),
        P("dp"),
        P("dp", None, None),
        P("section", None, "chan"),
        P("section", "chan", None),
        P("section", "chan"),
        P("section", "chan", None),
        P("chan"),
        P("chan", "dp", None, None),
    )
    out_specs = (
        P("chan", "dp", None, None),
        P("dp", "section", None, "chan"),
        P("section", None, "chan"),
        P("section", "chan", None),
        P("section", "chan"),
        P("section", "chan", None),
        P("chan"),
    )
    return jax.shard_map(local, mesh=mesh, in_specs=in_specs, out_specs=out_specs, check_vma=False)
```

```python
import math

import jax
import jax.numpy as jnp
from jax import lax
from jax.experimental import pallas as pl
from jax.experimental.pallas import tpu as pltpu
from jax.sharding import PartitionSpec as P

RATE = 6
BAND = 64
VOID = 19
LANES = 128
VMEM_LIMIT = 56 * 1024 * 1024
VECTOR_COST = 3800


def swish_slope(value):
    sig = jax.nn.sigmoid(value)
    return sig * (1.0 + value * (1.0 - sig))


def column_masks(first, step, count, cols):
    place = lax.broadcasted_iota(jnp.int32, (count, LANES), 0) + first
    place = jnp.where(place >= cols, place - cols, place)
    place = jnp.where(place < 0, place + cols, place)
    lower = (place - step >= 0).astype(jnp.float32)
    upper = (place + step < cols).astype(jnp.float32)
    return lower, upper


def tap_rows(taps, g):
    kernel = taps[:, g * LANES:(g + 1) * LANES].astype(jnp.float32)
    return [jnp.broadcast_to(kernel[t:t + 1], (8, LANES))[None] for t in range(9)]


def forward_kernel(scal, feats, taps, weight, depth, band, pre, masked, doubled, left, middle, right, edges, *, margin, wing, batch):
    rows, cols, chans = feats.shape[1:]
    ext = depth.shape[1]
    off, width, rate = scal[0], scal[1], scal[2]
    groups = [pl.ds(g * LANES, LANES) for g in range(chans // LANES)]

    @pl.when(pl.program_id(0) == 0)
    def _():
        masked[...] = jnp.zeros_like(masked)
        left[...] = jnp.zeros_like(left)
        middle[...] = jnp.zeros_like(middle)
        right[...] = jnp.zeros_like(right)
        pre[...] = jnp.zeros_like(pre)
        lower, upper = column_masks(off - wing, rate, ext, cols)
        edges[0] = lower
        edges[1] = upper

    def fill(i, carry):
        for k in range(batch):
            for g, lanes in enumerate(groups):
                row = feats[0, i * batch + k, :, lanes].astype(jnp.float32)
                doubled[k, g, 0:cols] = row
                doubled[k, g, cols:cols + BAND] = row[0:BAND]
        inside = (lax.broadcasted_iota(jnp.int32, (BAND, LANES), 0) < width).astype(jnp.float32)
        for k in range(batch):
            h = i * batch + k
            for g, lanes in enumerate(groups):
                part = doubled[k, g, pl.ds(off, BAND)] * inside
                masked[g, margin + h] = part
                band[h, :, lanes] = part.astype(jnp.bfloat16)
        return carry

    lax.fori_loop(0, rows // batch, fill, 0)
    kernels = [tap_rows(taps, g) for g in range(len(groups))]

    def row_group(i, carry):
        for k in range(batch):
            h = i * batch + k
            for g in range(len(groups)):
                for u in range(0, BAND, 16):
                    sources = [
                        masked[g, h + margin + (t - 1) * rate, u:u + 16].reshape(2, 8, LANES) for t in range(3)
                    ]
                    sums = []
                    for j in range(3):
                        total = sources[0] * kernels[g][j]
                        for t in (1, 2):
                            total = total + sources[t] * kernels[g][3 * t + j]
                        sums.append(total.reshape(16, LANES))
                    left[k, g, 2 * wing + u:2 * wing + u + 16] = sums[0]
                    middle[k, g, wing + u:wing + u + 16] = sums[1]
                    right[k, g, wing + u:wing + u + 16] = sums[2]
        for k in range(batch):
            h = i * batch + k
            for g, lanes in enumerate(groups):
                for e in range(0, ext, 16):
                    from_left = left[k, g, pl.ds(wing - rate + e, 16)] * edges[0, e:e + 16]
                    from_right = right[k, g, pl.ds(rate + e, 16)] * edges[1, e:e + 16]
                    out = from_left + from_right + middle[k, g, e:e + 16]
                    depth[h, e:e + 16, lanes] = out.astype(jnp.bfloat16)
        some = depth[pl.ds(i * batch, batch)].reshape(batch * ext, chans)
        here = pl.ds(pl.multiple_of(i * batch * ext, 16), batch * ext)
        pre[here, :] += jnp.dot(some, weight[...], preferred_element_type=jnp.float32)
        return carry

    lax.fori_loop(0, rows // batch, row_group, 0)


def forward_call(scal, feats, taps, weight, frame, margin, wing):
    rows, cols, chans = feats.shape[1:]
    ext = BAND + 2 * wing
    block = min(256, chans)
    outs = weight.shape[1]
    buffer = 3 * wing + BAND
    batch = 4 if rows % 4 == 0 else 1
    lanes = block // LANES
    return pl.pallas_call(
        lambda *refs: forward_kernel(*refs, margin=margin, wing=wing, batch=batch),
        grid_spec=pltpu.PrefetchScalarGridSpec(
            num_scalar_prefetch=1,
            grid=(chans // block,),
            in_specs=[
                pl.BlockSpec((1, rows, cols, block), lambda c, s: (frame, 0, 0, c)),
                pl.BlockSpec((9, block), lambda c, s: (0, c)),
                pl.BlockSpec((block, outs), lambda c, s: (c, 0)),
            ],
            out_specs=[
                pl.BlockSpec((rows, ext, block), lambda c, s: (0, 0, c)),
                pl.BlockSpec((rows, BAND, block), lambda c, s: (0, 0, c)),
                pl.BlockSpec((rows * ext, outs), lambda c, s: (0, 0)),
            ],
            scratch_shapes=[
                pltpu.VMEM((lanes, rows + 2 * margin, BAND, LANES), jnp.float32),
                pltpu.VMEM((batch, lanes, cols + BAND, LANES), jnp.float32),
                pltpu.VMEM((batch, lanes, buffer, LANES), jnp.float32),
                pltpu.VMEM((batch, lanes, ext, LANES), jnp.float32),
                pltpu.VMEM((batch, lanes, buffer, LANES), jnp.float32),
                pltpu.VMEM((2, ext, LANES), jnp.float32),
            ],
        ),
        out_shape=[
            jax.ShapeDtypeStruct((rows, ext, chans), jnp.bfloat16),
            jax.ShapeDtypeStruct((rows, BAND, chans), jnp.bfloat16),
            jax.ShapeDtypeStruct((rows * ext, outs), jnp.float32),
        ],
        compiler_params=pltpu.CompilerParams(vmem_limit_bytes=VMEM_LIMIT),
        cost_estimate=pl.CostEstimate(
            flops=VECTOR_COST * 3 * rows * BAND * chans, bytes_accessed=2 * rows * chans * (cols + ext + BAND), transcendentals=0
        ),
        name="depth_pointwise",
    )(scal, feats, taps, weight)


def backward_kernel(scal, grad, weight, taps, band, term, dw, spread, valid, *, margin, wing):
    rows, ext, outs = grad.shape
    chans = weight.shape[0]
    cols = scal[3]
    off, width, rate = scal[0], scal[1], scal[2]
    batch = 4 if rows % 4 == 0 else 1

    @pl.when(pl.program_id(0) == 0)
    def _():
        spread[...] = jnp.zeros_like(spread)
        lower, upper = column_masks(off, rate, BAND, cols)
        inside = (lax.broadcasted_iota(jnp.int32, (BAND, LANES), 0) < width).astype(jnp.float32)
        valid[0] = upper * inside
        valid[1] = inside
        valid[2] = lower * inside

    def product(i, carry):
        some = grad[pl.ds(i * batch, batch)].reshape(batch * ext, outs)
        out = lax.dot_general(some, weight[...], (((1,), (1,)), ((), ())), preferred_element_type=jnp.float32)
        out = out.astype(jnp.bfloat16).astype(jnp.float32).reshape(batch, ext, chans)
        for g in range(chans // LANES):
            spread[g, pl.ds(margin + i * batch, batch)] = out[:, :, g * LANES:(g + 1) * LANES]
        return carry

    lax.fori_loop(0, rows // batch, product, 0)

    for g in range(chans // LANES):
        lanes = pl.ds(g * LANES, LANES)
        kernel = tap_rows(taps, g)

        def one_row(h, sums):
            sums = list(sums)
            for u in range(0, BAND, 16):
                here = band[h, u:u + 16, lanes].astype(jnp.float32).reshape(2, 8, LANES)
                total = None
                for j in range(3):
                    mask = valid[j, u:u + 16].reshape(2, 8, LANES)
                    source = here * mask if j != 1 else here
                    part = None
                    for t in range(3):
                        value = spread[g, h + margin - (t - 1) * rate, pl.ds(wing - (j - 1) * rate + u, 16)]
                        value = value.reshape(2, 8, LANES)
                        both = source * value
                        sums[3 * t + j] = sums[3 * t + j] + (both[0] + both[1])
                        scaled = value * kernel[3 * t + j]
                        part = scaled if part is None else part + scaled
                    part = part * mask
                    total = part if total is None else total + part
                term[h, u:u + 16, lanes] = total.reshape(16, LANES).astype(jnp.bfloat16)
            return tuple(sums)

        sums = lax.fori_loop(0, rows, one_row, tuple(jnp.zeros((8, LANES), jnp.float32) for _ in range(9)))
        for t in range(9):
            dw[t:t + 1, lanes] = jnp.sum(sums[t], axis=0, keepdims=True)


def backward_call(scal, grad, weight, taps, band, margin, wing, cut, cuts):
    rows, ext, outs = grad.shape
    chans = weight.shape[0] // cuts
    block = min(256, chans)
    first = cut * (chans // block)
    return pl.pallas_call(
        lambda *refs: backward_kernel(*refs, margin=margin, wing=wing),
        grid_spec=pltpu.PrefetchScalarGridSpec(
            num_scalar_prefetch=1,
            grid=(chans // block,),
            in_specs=[
                pl.BlockSpec((rows, ext, outs), lambda c, s: (0, 0, 0)),
                pl.BlockSpec((block, outs), lambda c, s: (first + c, 0)),
                pl.BlockSpec((9, block), lambda c, s: (0, first + c)),
                pl.BlockSpec((rows, BAND, block), lambda c, s: (0, 0, first + c)),
            ],
            out_specs=[
                pl.BlockSpec((rows, BAND, block), lambda c, s: (0, 0, c)),
                pl.BlockSpec((9, block), lambda c, s: (0, c)),
            ],
            scratch_shapes=[
                pltpu.VMEM((block // LANES, rows + 2 * margin, ext, LANES), jnp.float32),
                pltpu.VMEM((3, BAND, LANES), jnp.float32),
            ],
        ),
        out_shape=[
            jax.ShapeDtypeStruct((rows, BAND, chans), jnp.bfloat16),
            jax.ShapeDtypeStruct((9, chans), jnp.float32),
        ],
        compiler_params=pltpu.CompilerParams(vmem_limit_bytes=VMEM_LIMIT),
        cost_estimate=pl.CostEstimate(
            flops=VECTOR_COST * 4 * rows * BAND * chans, bytes_accessed=8 * rows * chans * BAND, transcendentals=0
        ),
        name="depth_gradients",
    )(scal, grad, weight, taps, band)


def pick(array, index, axis=0):
    return lax.dynamic_index_in_dim(array, index, axis, keepdims=False)


def owner_terms(blocks, axis):
    size, me = lax.axis_size(axis), lax.axis_index(axis)
    terms = []
    for k in range(1, size):
        sent = pick(blocks, lax.rem(me + k, size)).astype(jnp.bfloat16)
        terms.append(lax.ppermute(sent, axis, [(i, (i + k) % size) for i in range(size)]))
    return terms


def owner_total(blocks, terms, axis):
    total = pick(blocks, lax.axis_index(axis)).astype(jnp.float32)
    for term in terms:
        total = total + term.astype(jnp.float32)
    return total


def owner_sum(blocks, axis):
    return owner_total(blocks, owner_terms(blocks, axis), axis)


def trade(blocks, axis):
    size, me = lax.axis_size(axis), lax.axis_index(axis)
    result = blocks
    for k in range(1, size):
        sent = pick(blocks, lax.rem(me + k, size))
        got = lax.ppermute(sent, axis, [(i, (i + k) % size) for i in range(size)])
        result = lax.dynamic_update_index_in_dim(result, got, lax.rem(me + size - k, size), 0)
    return result


def gather(block, axis):
    size, me = lax.axis_size(axis), lax.axis_index(axis)
    if size == 2:
        got = lax.ppermute(block, axis, [(0, 1), (1, 0)])
        return jnp.where(me == 0, jnp.stack([block, got]), jnp.stack([got, block]))
    return lax.all_gather(block, axis)


def halving_step(blocks, axis, bit):
    size, me = lax.axis_size(axis), lax.axis_index(axis)
    blocks = blocks.reshape((blocks.shape[0] // 2, 2) + blocks.shape[1:])
    mine = lax.rem(me // bit, 2)
    sent = pick(blocks, 1 - mine, 1).astype(jnp.bfloat16)
    got = lax.ppermute(sent, axis, [(i, i ^ bit) for i in range(size)])
    return pick(blocks, mine, 1).astype(jnp.float32) + got.astype(jnp.float32)


def halving_rest(blocks, axis, bit):
    while bit < lax.axis_size(axis):
        blocks = halving_step(blocks, axis, bit)
        bit *= 2
    return blocks[0]


def halving_sum(blocks, axis):
    return halving_rest(blocks, axis, 1)


def doubling_gather(block, axis, bit=None, last=1):
    size, me = lax.axis_size(axis), lax.axis_index(axis)
    if bit is None:
        bit, block = size // 2, block[None]
    shape = block.shape[1:]
    while bit >= last:
        got = lax.ppermute(block, axis, [(i, i ^ bit) for i in range(size)])
        mine = lax.rem(me // bit, 2)
        both = jnp.where(mine == 0, jnp.stack([block, got], 1), jnp.stack([got, block], 1))
        block = both.reshape((2 * block.shape[0],) + shape)
        bit //= 2
    return block


def butterfly_sum(value, axis):
    size, bit = lax.axis_size(axis), 1
    while bit < size:
        value = value + lax.ppermute(value, axis, [(i, i ^ bit) for i in range(size)])
        bit *= 2
    return value


def rolled(array, start, axis):
    length = array.shape[axis]
    return lax.dynamic_slice_in_dim(jnp.concatenate([array, array], axis), start, length, axis)


def local(feats, offsets, widths, labels, dw_kernel, pw_weight, pw_bias, proj, proj_bias, upstream):
    frames, rows, cols, chans = feats.shape
    sections, parts = lax.axis_size("section"), lax.axis_size("chan")
    section, part = lax.axis_index("section"), lax.axis_index("chan")
    rate = (RATE * section).astype(jnp.int32)
    margin = RATE * (sections - 1)
    wing = -(-margin // 8) * 8
    ext = BAND + 2 * wing
    share = pw_bias.shape[1]
    branch = share * parts
    scaling = 1.0 / math.sqrt(frames * rows * cols * lax.axis_size("dp"))
    rows_own = rows // parts
    pixels = rows_own * cols
    piece = pixels // sections
    taps, weight = dw_kernel[0], pw_weight[0]

    proj_all = gather(proj[0], "chan").reshape(branch, branch)
    biases = gather(jnp.stack([pw_bias[0], proj_bias]), "chan")
    pw_bias_all, proj_bias_all = biases[:, 0].reshape(branch), biases[:, 1].reshape(branch)

    starts = [lax.rem(offsets[f] + (cols - wing), cols) for f in range(frames)]
    scals = [jnp.stack([offsets[f], widths[f], rate, jnp.int32(cols)]) for f in range(frames)]

    firsts = [forward_call(scals[0], feats, taps, weight, 0, margin, wing)]
    for f in range(1, frames):
        scal, proj_all, pw_bias_all, proj_bias_all = lax.optimization_barrier(
            (scals[f], proj_all, pw_bias_all, proj_bias_all)
        )
        firsts.append(forward_call(scal, feats, taps, weight, f, margin, wing))

    _, upstream, labels = lax.optimization_barrier((firsts[0][2], upstream, labels))
    ups, labeled = [], []
    for f in range(frames):
        up = rolled(upstream[:, f], starts[f], 2).reshape(share, parts, sections, piece)
        up = pick(up, section, 2).transpose(1, 0, 2)
        ups.append(trade(up, "chan").reshape(branch, piece).T)
        marks = rolled(labels[f], starts[f], 1).reshape(parts, sections, piece)
        labeled.append((pick(pick(marks, part), section) != VOID).astype(jnp.float32))

    pre_grad = firsts[-1][2]
    blocked = [first[2].reshape(parts, rows_own * ext, branch) for first in firsts]
    terms = [owner_terms(blocks, "chan") for blocks in blocked]
    kept, grads, outs = [], [], []
    proj_sum = pw_bias_sum = proj_bias_sum = 0.0
    for f in range(frames):
        blocks, arrived, _ = lax.optimization_barrier((blocked[f], terms[f], pre_grad))
        own = owner_total(blocks, arrived, "chan") + pw_bias_all
        rest = jnp.broadcast_to(pw_bias_all, (rows_own, cols - ext, branch))
        preact = jnp.concatenate([own.reshape(rows_own, ext, branch), rest], axis=1).reshape(pixels, branch)
        act = jax.nn.silu(preact).astype(jnp.bfloat16)
        zpart = jnp.dot(act, proj_all, preferred_element_type=jnp.float32)
        zvalue = halving_sum(zpart.reshape(sections, piece, branch), "section") + proj_bias_all
        if f + 1 < frames:
            zvalue, terms[f + 1] = lax.optimization_barrier((zvalue, terms[f + 1]))
        outs.append(jax.nn.silu(zvalue).astype(jnp.bfloat16))
        out_grad = ups[f].astype(jnp.float32) * swish_slope(zvalue) * labeled[f][:, None]
        out_grad = doubling_gather(out_grad.astype(jnp.bfloat16), "section").reshape(pixels, branch)
        act_grad = lax.dot_general(out_grad, proj_all, (((1,), (1,)), ((), ())), preferred_element_type=jnp.float32)
        pre_grad = (act_grad * swish_slope(preact)).astype(jnp.bfloat16)
        sent = pre_grad.reshape(rows_own, cols, branch)[:, :ext]
        grads.append(gather(sent, "chan").reshape(rows, ext, branch))
        kept.append(lax.optimization_barrier((act, out_grad, pre_grad)))

    outs, grads[0], _ = lax.optimization_barrier((outs, grads[0], pre_grad))
    pw_sum = 0.0
    for f in range(frames):
        act, out_grad, pre_grad = kept[f]
        pw_sum = pw_sum + lax.dot_general(
            firsts[f][0].reshape(rows * ext, chans), grads[f].reshape(rows * ext, branch),
            (((0,), (0,)), ((), ())), preferred_element_type=jnp.float32,
        )
        proj_sum = proj_sum + lax.dot_general(
            act, out_grad, (((0,), (0,)), ((), ())), preferred_element_type=jnp.float32
        )
        pw_bias_sum = pw_bias_sum + jnp.sum(pre_grad.astype(jnp.float32), axis=0)
        proj_bias_sum = proj_bias_sum + jnp.sum(out_grad.astype(jnp.float32), axis=0)
    proj_rows = owner_sum(proj_sum.reshape(parts, share, branch), "chan")
    bias_rows = jnp.stack([pw_bias_sum, proj_bias_sum]).reshape(2, parts, share).transpose(1, 0, 2)
    bias_rows = owner_sum(bias_rows, "chan")
    bias_rows = jnp.pad(bias_rows, ((0, 6), (0, branch - share)))
    shared = jnp.concatenate([pw_sum, proj_rows, bias_rows], axis=0) * scaling
    depth_count = lax.axis_size("dp")
    shared = shared.reshape(depth_count, shared.shape[0] // depth_count, branch)
    swapped = [trade(outs[f].reshape(piece, parts, share).transpose(1, 2, 0), "chan") for f in range(frames)]

    def first_step(term):
        term = term.reshape((sections, rows // sections) + term.shape[1:])
        return halving_step(term, "section", 1)

    stepped, dw_sum = [], 0.0
    for f in range(frames - 1):
        term, dw = backward_call(scals[f], grads[f], weight, taps, firsts[f][1], margin, wing, 0, 1)
        stepped.append([first_step(term)])
        dw_sum = dw_sum + dw
    last = grads[-1]
    last, stepped, shared, swapped = lax.optimization_barrier((last, stepped, shared, swapped))
    shared = halving_step(shared, "dp", 1)
    spreads = [doubling_gather(swapped[f][None], "section", sections // 2, 2) for f in range(frames)]
    summed = [[halving_rest(part, "section", 2) for part in parts_of] for parts_of in stepped]
    cuts = 2 if chans % 512 == 0 else 1
    final, dw_last = [], []
    for cut in range(cuts):
        if cut:
            last, shared, spreads, summed, term = lax.optimization_barrier((last, shared, spreads, summed, term))
            final.append(first_step(term))
        term, dw = backward_call(scals[-1], last, weight, taps, firsts[-1][1], margin, wing, cut, cuts)
        dw_last.append(dw)
    final.append(first_step(term))
    summed.append([halving_rest(part, "section", 2) for part in final])
    shared = halving_rest(shared, "dp", 2).astype(jnp.bfloat16)
    shared = doubling_gather(shared, "dp").reshape(-1, branch).astype(jnp.float32)
    kernel_grad = butterfly_sum((dw_sum + jnp.concatenate(dw_last, axis=1)) * scaling, "dp")

    terms, results = [], []
    for f in range(frames):
        own_rows = jnp.concatenate(summed[f], axis=2).astype(jnp.bfloat16)
        own_rows = jnp.pad(own_rows, ((0, 0), (0, cols - BAND), (0, 0)))
        terms.append(rolled(own_rows, lax.rem(cols - offsets[f], cols), 1))
        whole = doubling_gather(spreads[f], "section", 1).transpose(2, 1, 0, 3).reshape(share, rows, cols)
        results.append(rolled(whole, lax.rem(cols - starts[f], cols), 2))

    proj_end = chans + share
    return (
        jnp.stack(results, 1),
        jnp.stack(terms, 0),
        kernel_grad[None],
        shared[None, :chans],
        shared[proj_end:proj_end + 1, :share],
        shared[None, chans:proj_end],
        shared[proj_end + 1, :share],
    )


def solution(mesh):
    in_specs = (
        P("dp", None, None, "chan"),
        P("dp"),
        P("dp"),
        P("dp", None, None),
        P("section", None, "chan"),
        P("section", "chan", None),
        P("section", "chan"),
        P("section", "chan", None),
        P("chan"),
        P("chan", "dp", None, None),
    )
    out_specs = (
        P("chan", "dp", None, None),
        P("dp", "section", None, "chan"),
        P("section", None, "chan"),
        P("section", "chan", None),
        P("section", "chan"),
        P("section", "chan", None),
        P("chan"),
    )
    return jax.shard_map(local, mesh=mesh, in_specs=in_specs, out_specs=out_specs, check_vma=False)
```

```python
import math

import jax
import jax.numpy as jnp
from jax import lax
from jax.experimental import pallas as pl
from jax.experimental.pallas import tpu as pltpu
from jax.sharding import PartitionSpec as P

RATE = 6
BAND = 64
VOID = 19
LANES = 128
VMEM_LIMIT = 56 * 1024 * 1024
VECTOR_COST = 3800


def swish_slope(value):
    sig = jax.nn.sigmoid(value)
    return sig * (1.0 + value * (1.0 - sig))


def column_masks(first, step, count, cols):
    place = lax.broadcasted_iota(jnp.int32, (count, LANES), 0) + first
    place = jnp.where(place >= cols, place - cols, place)
    place = jnp.where(place < 0, place + cols, place)
    lower = (place - step >= 0).astype(jnp.float32)
    upper = (place + step < cols).astype(jnp.float32)
    return lower, upper


def tap_rows(taps, g):
    kernel = taps[:, g * LANES:(g + 1) * LANES].astype(jnp.float32)
    return [jnp.broadcast_to(kernel[t:t + 1], (8, LANES))[None] for t in range(9)]


def forward_kernel(scal, feats, taps, weight, depth, band, pre, masked, doubled, left, middle, right, edges, *, margin, wing, batch):
    rows, cols, chans = feats.shape[1:]
    ext = depth.shape[1]
    off, width, rate = scal[0], scal[1], scal[2]
    groups = [pl.ds(g * LANES, LANES) for g in range(chans // LANES)]

    @pl.when(pl.program_id(0) == 0)
    def _():
        masked[...] = jnp.zeros_like(masked)
        left[...] = jnp.zeros_like(left)
        middle[...] = jnp.zeros_like(middle)
        right[...] = jnp.zeros_like(right)
        pre[...] = jnp.zeros_like(pre)
        lower, upper = column_masks(off - wing, rate, ext, cols)
        edges[0] = lower
        edges[1] = upper

    def fill(i, carry):
        for k in range(batch):
            for g, lanes in enumerate(groups):
                row = feats[0, i * batch + k, :, lanes].astype(jnp.float32)
                doubled[k, g, 0:cols] = row
                doubled[k, g, cols:cols + BAND] = row[0:BAND]
        inside = (lax.broadcasted_iota(jnp.int32, (BAND, LANES), 0) < width).astype(jnp.float32)
        for k in range(batch):
            h = i * batch + k
            for g, lanes in enumerate(groups):
                part = doubled[k, g, pl.ds(off, BAND)] * inside
                masked[g, margin + h] = part
                band[h, :, lanes] = part.astype(jnp.bfloat16)
        return carry

    lax.fori_loop(0, rows // batch, fill, 0)
    kernels = [tap_rows(taps, g) for g in range(len(groups))]

    def row_group(i, carry):
        for k in range(batch):
            h = i * batch + k
            for g in range(len(groups)):
                for u in range(0, BAND, 16):
                    sources = [
                        masked[g, h + margin + (t - 1) * rate, u:u + 16].reshape(2, 8, LANES) for t in range(3)
                    ]
                    sums = []
                    for j in range(3):
                        total = sources[0] * kernels[g][j]
                        for t in (1, 2):
                            total = total + sources[t] * kernels[g][3 * t + j]
                        sums.append(total.reshape(16, LANES))
                    left[k, g, 2 * wing + u:2 * wing + u + 16] = sums[0]
                    middle[k, g, wing + u:wing + u + 16] = sums[1]
                    right[k, g, wing + u:wing + u + 16] = sums[2]
        for k in range(batch):
            h = i * batch + k
            for g, lanes in enumerate(groups):
                for e in range(0, ext, 16):
                    from_left = left[k, g, pl.ds(wing - rate + e, 16)] * edges[0, e:e + 16]
                    from_right = right[k, g, pl.ds(rate + e, 16)] * edges[1, e:e + 16]
                    out = from_left + from_right + middle[k, g, e:e + 16]
                    depth[h, e:e + 16, lanes] = out.astype(jnp.bfloat16)
        some = depth[pl.ds(i * batch, batch)].reshape(batch * ext, chans)
        here = pl.ds(pl.multiple_of(i * batch * ext, 16), batch * ext)
        pre[here, :] += jnp.dot(some, weight[...], preferred_element_type=jnp.float32)
        return carry

    lax.fori_loop(0, rows // batch, row_group, 0)


def forward_call(scal, feats, taps, weight, frame, margin, wing):
    rows, cols, chans = feats.shape[1:]
    ext = BAND + 2 * wing
    block = min(256, chans)
    outs = weight.shape[1]
    buffer = 3 * wing + BAND
    batch = 4 if rows % 4 == 0 else 1
    lanes = block // LANES
    return pl.pallas_call(
        lambda *refs: forward_kernel(*refs, margin=margin, wing=wing, batch=batch),
        grid_spec=pltpu.PrefetchScalarGridSpec(
            num_scalar_prefetch=1,
            grid=(chans // block,),
            in_specs=[
                pl.BlockSpec((1, rows, cols, block), lambda c, s: (frame, 0, 0, c)),
                pl.BlockSpec((9, block), lambda c, s: (0, c)),
                pl.BlockSpec((block, outs), lambda c, s: (c, 0)),
            ],
            out_specs=[
                pl.BlockSpec((rows, ext, block), lambda c, s: (0, 0, c)),
                pl.BlockSpec((rows, BAND, block), lambda c, s: (0, 0, c)),
                pl.BlockSpec((rows * ext, outs), lambda c, s: (0, 0)),
            ],
            scratch_shapes=[
                pltpu.VMEM((lanes, rows + 2 * margin, BAND, LANES), jnp.float32),
                pltpu.VMEM((batch, lanes, cols + BAND, LANES), jnp.float32),
                pltpu.VMEM((batch, lanes, buffer, LANES), jnp.float32),
                pltpu.VMEM((batch, lanes, ext, LANES), jnp.float32),
                pltpu.VMEM((batch, lanes, buffer, LANES), jnp.float32),
                pltpu.VMEM((2, ext, LANES), jnp.float32),
            ],
        ),
        out_shape=[
            jax.ShapeDtypeStruct((rows, ext, chans), jnp.bfloat16),
            jax.ShapeDtypeStruct((rows, BAND, chans), jnp.bfloat16),
            jax.ShapeDtypeStruct((rows * ext, outs), jnp.float32),
        ],
        compiler_params=pltpu.CompilerParams(vmem_limit_bytes=VMEM_LIMIT),
        cost_estimate=pl.CostEstimate(
            flops=VECTOR_COST * 3 * rows * BAND * chans, bytes_accessed=2 * rows * chans * (cols + ext + BAND), transcendentals=0
        ),
        name="depth_pointwise",
    )(scal, feats, taps, weight)


def backward_kernel(scal, grad, weight, taps, band, term, dw, spread, valid, *, margin, wing):
    rows, ext, outs = grad.shape
    chans = weight.shape[0]
    cols = scal[3]
    off, width, rate = scal[0], scal[1], scal[2]
    batch = 4 if rows % 4 == 0 else 1

    @pl.when(pl.program_id(0) == 0)
    def _():
        spread[...] = jnp.zeros_like(spread)
        lower, upper = column_masks(off, rate, BAND, cols)
        inside = (lax.broadcasted_iota(jnp.int32, (BAND, LANES), 0) < width).astype(jnp.float32)
        valid[0] = upper * inside
        valid[1] = inside
        valid[2] = lower * inside

    def product(i, carry):
        some = grad[pl.ds(i * batch, batch)].reshape(batch * ext, outs)
        out = lax.dot_general(some, weight[...], (((1,), (1,)), ((), ())), preferred_element_type=jnp.float32)
        out = out.astype(jnp.bfloat16).astype(jnp.float32).reshape(batch, ext, chans)
        for g in range(chans // LANES):
            spread[g, pl.ds(margin + i * batch, batch)] = out[:, :, g * LANES:(g + 1) * LANES]
        return carry

    lax.fori_loop(0, rows // batch, product, 0)

    for g in range(chans // LANES):
        lanes = pl.ds(g * LANES, LANES)
        kernel = tap_rows(taps, g)

        def one_row(h, sums):
            sums = list(sums)
            for u in range(0, BAND, 16):
                here = band[h, u:u + 16, lanes].astype(jnp.float32).reshape(2, 8, LANES)
                total = None
                for j in range(3):
                    mask = valid[j, u:u + 16].reshape(2, 8, LANES)
                    source = here * mask if j != 1 else here
                    part = None
                    for t in range(3):
                        value = spread[g, h + margin - (t - 1) * rate, pl.ds(wing - (j - 1) * rate + u, 16)]
                        value = value.reshape(2, 8, LANES)
                        both = source * value
                        sums[3 * t + j] = sums[3 * t + j] + (both[0] + both[1])
                        scaled = value * kernel[3 * t + j]
                        part = scaled if part is None else part + scaled
                    part = part * mask
                    total = part if total is None else total + part
                term[h, u:u + 16, lanes] = total.reshape(16, LANES).astype(jnp.bfloat16)
            return tuple(sums)

        sums = lax.fori_loop(0, rows, one_row, tuple(jnp.zeros((8, LANES), jnp.float32) for _ in range(9)))
        for t in range(9):
            dw[t:t + 1, lanes] = jnp.sum(sums[t], axis=0, keepdims=True)


def backward_call(scal, grad, weight, taps, band, margin, wing, cut, cuts):
    rows, ext, outs = grad.shape
    chans = weight.shape[0] // cuts
    block = min(256, chans)
    first = cut * (chans // block)
    return pl.pallas_call(
        lambda *refs: backward_kernel(*refs, margin=margin, wing=wing),
        grid_spec=pltpu.PrefetchScalarGridSpec(
            num_scalar_prefetch=1,
            grid=(chans // block,),
            in_specs=[
                pl.BlockSpec((rows, ext, outs), lambda c, s: (0, 0, 0)),
                pl.BlockSpec((block, outs), lambda c, s: (first + c, 0)),
                pl.BlockSpec((9, block), lambda c, s: (0, first + c)),
                pl.BlockSpec((rows, BAND, block), lambda c, s: (0, 0, first + c)),
            ],
            out_specs=[
                pl.BlockSpec((rows, BAND, block), lambda c, s: (0, 0, c)),
                pl.BlockSpec((9, block), lambda c, s: (0, c)),
            ],
            scratch_shapes=[
                pltpu.VMEM((block // LANES, rows + 2 * margin, ext, LANES), jnp.float32),
                pltpu.VMEM((3, BAND, LANES), jnp.float32),
            ],
        ),
        out_shape=[
            jax.ShapeDtypeStruct((rows, BAND, chans), jnp.bfloat16),
            jax.ShapeDtypeStruct((9, chans), jnp.float32),
        ],
        compiler_params=pltpu.CompilerParams(vmem_limit_bytes=VMEM_LIMIT),
        cost_estimate=pl.CostEstimate(
            flops=VECTOR_COST * 4 * rows * BAND * chans, bytes_accessed=8 * rows * chans * BAND, transcendentals=0
        ),
        name="depth_gradients",
    )(scal, grad, weight, taps, band)


def pick(array, index, axis=0):
    return lax.dynamic_index_in_dim(array, index, axis, keepdims=False)


def owner_terms(blocks, axis):
    size, me = lax.axis_size(axis), lax.axis_index(axis)
    terms = []
    for k in range(1, size):
        sent = pick(blocks, lax.rem(me + k, size)).astype(jnp.bfloat16)
        terms.append(lax.ppermute(sent, axis, [(i, (i + k) % size) for i in range(size)]))
    return terms


def owner_total(blocks, terms, axis):
    total = pick(blocks, lax.axis_index(axis)).astype(jnp.float32)
    for term in terms:
        total = total + term.astype(jnp.float32)
    return total


def owner_sum(blocks, axis):
    return owner_total(blocks, owner_terms(blocks, axis), axis)


def trade(blocks, axis):
    size, me = lax.axis_size(axis), lax.axis_index(axis)
    result = blocks
    for k in range(1, size):
        sent = pick(blocks, lax.rem(me + k, size))
        got = lax.ppermute(sent, axis, [(i, (i + k) % size) for i in range(size)])
        result = lax.dynamic_update_index_in_dim(result, got, lax.rem(me + size - k, size), 0)
    return result


def gather(block, axis):
    size, me = lax.axis_size(axis), lax.axis_index(axis)
    if size == 2:
        got = lax.ppermute(block, axis, [(0, 1), (1, 0)])
        return jnp.where(me == 0, jnp.stack([block, got]), jnp.stack([got, block]))
    return lax.all_gather(block, axis)


def halving_step(blocks, axis, bit):
    size, me = lax.axis_size(axis), lax.axis_index(axis)
    blocks = blocks.reshape((blocks.shape[0] // 2, 2) + blocks.shape[1:])
    mine = lax.rem(me // bit, 2)
    sent = pick(blocks, 1 - mine, 1).astype(jnp.bfloat16)
    got = lax.ppermute(sent, axis, [(i, i ^ bit) for i in range(size)])
    return pick(blocks, mine, 1).astype(jnp.float32) + got.astype(jnp.float32)


def halving_rest(blocks, axis, bit):
    while bit < lax.axis_size(axis):
        blocks = halving_step(blocks, axis, bit)
        bit *= 2
    return blocks[0]


def halving_sum(blocks, axis):
    return halving_rest(blocks, axis, 1)


def doubling_gather(block, axis, bit=None, last=1):
    size, me = lax.axis_size(axis), lax.axis_index(axis)
    if bit is None:
        bit, block = size // 2, block[None]
    shape = block.shape[1:]
    while bit >= last:
        got = lax.ppermute(block, axis, [(i, i ^ bit) for i in range(size)])
        mine = lax.rem(me // bit, 2)
        both = jnp.where(mine == 0, jnp.stack([block, got], 1), jnp.stack([got, block], 1))
        block = both.reshape((2 * block.shape[0],) + shape)
        bit //= 2
    return block


def butterfly_sum(value, axis):
    size, bit = lax.axis_size(axis), 1
    while bit < size:
        value = value + lax.ppermute(value, axis, [(i, i ^ bit) for i in range(size)])
        bit *= 2
    return value


def rolled(array, start, axis):
    length = array.shape[axis]
    return lax.dynamic_slice_in_dim(jnp.concatenate([array, array], axis), start, length, axis)


def local(feats, offsets, widths, labels, dw_kernel, pw_weight, pw_bias, proj, proj_bias, upstream):
    frames, rows, cols, chans = feats.shape
    sections, parts = lax.axis_size("section"), lax.axis_size("chan")
    section, part = lax.axis_index("section"), lax.axis_index("chan")
    rate = (RATE * section).astype(jnp.int32)
    margin = RATE * (sections - 1)
    wing = -(-margin // 8) * 8
    ext = BAND + 2 * wing
    share = pw_bias.shape[1]
    branch = share * parts
    scaling = 1.0 / math.sqrt(frames * rows * cols * lax.axis_size("dp"))
    rows_own = rows // parts
    pixels = rows_own * cols
    piece = pixels // sections
    taps, weight = dw_kernel[0], pw_weight[0]

    proj_all = gather(proj[0], "chan").reshape(branch, branch)
    biases = gather(jnp.stack([pw_bias[0], proj_bias]), "chan")
    pw_bias_all, proj_bias_all = biases[:, 0].reshape(branch), biases[:, 1].reshape(branch)

    starts = [lax.rem(offsets[f] + (cols - wing), cols) for f in range(frames)]
    scals = [jnp.stack([offsets[f], widths[f], rate, jnp.int32(cols)]) for f in range(frames)]

    firsts = [forward_call(scals[0], feats, taps, weight, 0, margin, wing)]
    for f in range(1, frames):
        scal, proj_all, pw_bias_all, proj_bias_all = lax.optimization_barrier(
            (scals[f], proj_all, pw_bias_all, proj_bias_all)
        )
        firsts.append(forward_call(scal, feats, taps, weight, f, margin, wing))

    _, upstream, labels = lax.optimization_barrier((firsts[0][2], upstream, labels))
    ups, labeled = [], []
    for f in range(frames):
        up = rolled(upstream[:, f], starts[f], 2).reshape(share, parts, sections, piece)
        up = pick(up, section, 2).transpose(1, 0, 2)
        ups.append(trade(up, "chan").reshape(branch, piece).T)
        marks = rolled(labels[f], starts[f], 1).reshape(parts, sections, piece)
        labeled.append((pick(pick(marks, part), section) != VOID).astype(jnp.float32))

    pre_grad = firsts[-1][2]
    blocked = [first[2].reshape(parts, rows_own * ext, branch) for first in firsts]
    terms = [owner_terms(blocks, "chan") for blocks in blocked]
    kept, grads, outs = [], [], []
    proj_sum = pw_bias_sum = proj_bias_sum = 0.0
    for f in range(frames):
        blocks, arrived, _ = lax.optimization_barrier((blocked[f], terms[f], pre_grad))
        own = owner_total(blocks, arrived, "chan") + pw_bias_all
        rest = jnp.broadcast_to(pw_bias_all, (rows_own, cols - ext, branch))
        preact = jnp.concatenate([own.reshape(rows_own, ext, branch), rest], axis=1).reshape(pixels, branch)
        act = jax.nn.silu(preact).astype(jnp.bfloat16)
        zpart = jnp.dot(act, proj_all, preferred_element_type=jnp.float32)
        zvalue = halving_sum(zpart.reshape(sections, piece, branch), "section") + proj_bias_all
        if f + 1 < frames:
            zvalue, terms[f + 1] = lax.optimization_barrier((zvalue, terms[f + 1]))
        outs.append(jax.nn.silu(zvalue).astype(jnp.bfloat16))
        out_grad = ups[f].astype(jnp.float32) * swish_slope(zvalue) * labeled[f][:, None]
        out_grad = doubling_gather(out_grad.astype(jnp.bfloat16), "section").reshape(pixels, branch)
        act_grad = lax.dot_general(out_grad, proj_all, (((1,), (1,)), ((), ())), preferred_element_type=jnp.float32)
        pre_grad = (act_grad * swish_slope(preact)).astype(jnp.bfloat16)
        sent = pre_grad.reshape(rows_own, cols, branch)[:, :ext]
        grads.append(gather(sent, "chan").reshape(rows, ext, branch))
        kept.append(lax.optimization_barrier((act, out_grad, pre_grad)))

    outs, grads[0], _ = lax.optimization_barrier((outs, grads[0], pre_grad))
    pw_sum = 0.0
    for f in range(frames):
        act, out_grad, pre_grad = kept[f]
        pw_sum = pw_sum + lax.dot_general(
            firsts[f][0].reshape(rows * ext, chans), grads[f].reshape(rows * ext, branch),
            (((0,), (0,)), ((), ())), preferred_element_type=jnp.float32,
        )
        proj_sum = proj_sum + lax.dot_general(
            act, out_grad, (((0,), (0,)), ((), ())), preferred_element_type=jnp.float32
        )
        pw_bias_sum = pw_bias_sum + jnp.sum(pre_grad.astype(jnp.float32), axis=0)
        proj_bias_sum = proj_bias_sum + jnp.sum(out_grad.astype(jnp.float32), axis=0)
    proj_rows = owner_sum(proj_sum.reshape(parts, share, branch), "chan")
    bias_rows = jnp.stack([pw_bias_sum, proj_bias_sum]).reshape(2, parts, share).transpose(1, 0, 2)
    bias_rows = owner_sum(bias_rows, "chan")
    bias_rows = jnp.pad(bias_rows, ((0, 6), (0, branch - share)))
    shared = jnp.concatenate([pw_sum, proj_rows, bias_rows], axis=0) * scaling
    depth_count = lax.axis_size("dp")
    shared = shared.reshape(depth_count, shared.shape[0] // depth_count, branch)
    swapped = [trade(outs[f].reshape(piece, parts, share).transpose(1, 2, 0), "chan") for f in range(frames)]

    def first_step(term):
        term = term.reshape((sections, rows // sections) + term.shape[1:])
        return halving_step(term, "section", 1)

    stepped, dw_sum = [], 0.0
    for f in range(frames - 1):
        term, dw = backward_call(scals[f], grads[f], weight, taps, firsts[f][1], margin, wing, 0, 1)
        stepped.append([first_step(term)])
        dw_sum = dw_sum + dw
    last = grads[-1]
    last, stepped, shared, swapped = lax.optimization_barrier((last, stepped, shared, swapped))
    shared = halving_step(shared, "dp", 1)
    spreads = [doubling_gather(swapped[f][None], "section", sections // 2, 2) for f in range(frames)]
    summed = [[halving_rest(part, "section", 2) for part in parts_of] for parts_of in stepped]
    cuts = 2 if chans % 512 == 0 else 1
    final, dw_last = [], []
    for cut in range(cuts):
        if cut:
            last, shared, spreads, summed, term = lax.optimization_barrier((last, shared, spreads, summed, term))
            final.append(first_step(term))
        term, dw = backward_call(scals[-1], last, weight, taps, firsts[-1][1], margin, wing, cut, cuts)
        dw_last.append(dw)
    final.append(first_step(term))
    spreads, shared, final = lax.optimization_barrier((spreads, shared, final))
    summed.append([halving_rest(part, "section", 2) for part in final])
    shared = halving_rest(shared, "dp", 2).astype(jnp.bfloat16)
    shared = doubling_gather(shared, "dp").reshape(-1, branch).astype(jnp.float32)
    kernel_grad = butterfly_sum((dw_sum + jnp.concatenate(dw_last, axis=1)) * scaling, "dp")

    terms, results = [], []
    for f in range(frames):
        own_rows = jnp.concatenate(summed[f], axis=2).astype(jnp.bfloat16)
        own_rows = jnp.pad(own_rows, ((0, 0), (0, cols - BAND), (0, 0)))
        terms.append(rolled(own_rows, lax.rem(cols - offsets[f], cols), 1))
        whole = doubling_gather(spreads[f], "section", 1).transpose(2, 1, 0, 3).reshape(share, rows, cols)
        results.append(rolled(whole, lax.rem(cols - starts[f], cols), 2))

    proj_end = chans + share
    return (
        jnp.stack(results, 1),
        jnp.stack(terms, 0),
        kernel_grad[None],
        shared[None, :chans],
        shared[proj_end:proj_end + 1, :share],
        shared[None, chans:proj_end],
        shared[proj_end + 1, :share],
    )


def solution(mesh):
    in_specs = (
        P("dp", None, None, "chan"),
        P("dp"),
        P("dp"),
        P("dp", None, None),
        P("section", None, "chan"),
        P("section", "chan", None),
        P("section", "chan"),
        P("section", "chan", None),
        P("chan"),
        P("chan", "dp", None, None),
    )
    out_specs = (
        P("chan", "dp", None, None),
        P("dp", "section", None, "chan"),
        P("section", None, "chan"),
        P("section", "chan", None),
        P("section", "chan"),
        P("section", "chan", None),
        P("chan"),
    )
    return jax.shard_map(local, mesh=mesh, in_specs=in_specs, out_specs=out_specs, check_vma=False)
```
